32 devices in a mesh: groups: 2 (over x), rollout: 2 (over core), tensor: 8 (over z, y).
Axes of the slice: x: 2, y: 2, z: 4, core: 2. Of those that a mesh axis runs over, the one named last changes fastest.
Arguments:
- hidden_in: bfloat16 [128, 8192], P(('groups', 'tensor'), 'rollout'), parts along dimension 0, may hold values from -6 to 6
- norm_gain: float32 [8192], P('rollout'), may hold values from 0.1 to 1.9
- w_gate: bfloat16 [8192, 29568], P('rollout', 'tensor'), may hold values from -0.0625 to 0.0625
- w_up: bfloat16 [8192, 29568], P('rollout', 'tensor'), may hold values from -0.0625 to 0.0625
- w_down: bfloat16 [29568, 8192], P('tensor', 'rollout'), may hold values from -0.03125 to 0.03125
- width_factors: bfloat16 [6, 8192, 64], P('groups', ('rollout', 'tensor')), parts along dimension 0, may hold values from -0.0625 to 0.0625
- unit_factors: bfloat16 [6, 29568, 64], P('groups', ('rollout', 'tensor')), parts along dimension 0, may hold values from -1.5 to 1.5
- slot_block: int32 [32], P('groups'), parts along dimension 0, may hold values from 0 to 15, each once
Outputs:
- hidden_out: bfloat16 [128, 8192], P(('groups', 'tensor'), 'rollout'), parts along dimension 0
The draws below stay inside these ranges and needn't reach their ends.
There are 2 independent parts, one for each index of `groups`. The reference program is written for one: setup_inputs(seed, part) draws one part's arguments, and reference() takes and returns one part's arrays. A program takes and returns all parts, laid end to end along the dimension named above; an argument that names none is the same for every part. Nothing has to cross between parts.
Inputs may be any that keep to these rules, and one draw needn't show every extreme that they name: `slot_block`: each block number appears exactly once.
All inputs are finite; a program needn't handle non-finite values.
Results may differ from the reference program's by a relative error of at most 0.008.
Values may be sent and summed in bfloat16 or wider, within the bound.
A program may use at most 256 MiB of HBM per device.

```python
import jax
import jax.numpy as jnp
from jax import lax

D = 8192
FF = 29568
RANK = 64
ROWS = 64
BLOCKS = 16


def level_of(own_key, extent, split, least, largest):
    loudness = 1.0
    for dim, parts in split:
        heights = jax.random.uniform(jax.random.fold_in(jax.random.fold_in(own_key, 6), dim), (parts,), jnp.float32, least / len(split), largest / len(split))
        loudness = loudness * jnp.repeat(jnp.exp(heights), extent[dim] // parts).reshape((-1,) + (1,) * (len(extent) - 1 - dim))
    return loudness


def centred(own_key, shape, width, limit, shards=(), held_as=jnp.bfloat16):
    values = jax.random.normal(own_key, shape, jnp.float32) * width
    if len(shards) > 0:
        values = level_of(own_key, shape, shards, -0.22, 0.18) * values
    return jnp.clip(values, min=-limit, max=limit).astype(held_as)


def setup_inputs(seed: int = 0, part: int = 0) -> dict:
    arg_keys = jax.random.split(jax.random.key(seed), 9)
    own_keys = jax.random.split(jax.random.fold_in(arg_keys[8], part), 9)
    hidden_in = centred(own_keys[0], (ROWS, D), 1.0, 6.0, ((0, 8), (1, 2)))
    norm_gain = jnp.clip(1.0 + 0.18 * jax.random.normal(arg_keys[1], (D,), jnp.float32), 0.1, 1.9)
    w_gate = centred(arg_keys[2], (D, FF), D ** -0.5, 0.0625, ((0, 2), (1, 8)))
    w_up = centred(arg_keys[3], (D, FF), D ** -0.5, 0.0625, ((0, 2), (1, 8)))
    w_down = centred(arg_keys[4], (FF, D), FF ** -0.5, 0.03125, ((0, 8), (1, 2)))
    width_factors = centred(own_keys[5], (3, D, RANK), D ** -0.5, 0.0625, ((1, 16),))
    unit_factors = centred(own_keys[6], (3, FF, RANK), (RANK // 4) ** -0.5, 1.5, ((1, 16),))
    slot_block = jax.random.permutation(own_keys[7], BLOCKS).astype(jnp.int32)
    return {"hidden_in": hidden_in, "norm_gain": norm_gain, "w_gate": w_gate, "w_up": w_up, "w_down": w_down, "width_factors": width_factors, "unit_factors": unit_factors, "slot_block": slot_block}


def reference(hidden_in, norm_gain, w_gate, w_up, w_down, width_factors, unit_factors, slot_block):
    block = FF // BLOCKS
    stacked = unit_factors.reshape(3, BLOCKS, block, RANK)
    ordered = jnp.zeros_like(stacked).at[:, slot_block.astype(jnp.int32)].set(stacked).reshape(3, FF, RANK)
    gate_delta = jnp.dot(width_factors[0], ordered[0].T, preferred_element_type=jnp.float32)
    gate_merged = (w_gate.astype(jnp.float32) + 0.5 * gate_delta).astype(jnp.bfloat16)
    up_delta = jnp.dot(width_factors[1], ordered[1].T, preferred_element_type=jnp.float32)
    up_merged = (w_up.astype(jnp.float32) + 0.5 * up_delta).astype(jnp.bfloat16)
    down_delta = jnp.dot(ordered[2], width_factors[2].T, preferred_element_type=jnp.float32)
    down_merged = (w_down.astype(jnp.float32) + 0.5 * down_delta).astype(jnp.bfloat16)
    wide = hidden_in.astype(jnp.float32)
    power = lax.optimization_barrier(jnp.mean(wide * wide, axis=1, keepdims=True))
    normed = (wide * jax.lax.rsqrt(power + 1e-06) * norm_gain[None, :]).astype(jnp.bfloat16)
    gate = jnp.dot(normed, gate_merged, preferred_element_type=jnp.float32)
    upper = jnp.dot(normed, up_merged, preferred_element_type=jnp.float32)
    activated = (jax.nn.silu(gate) * upper).astype(jnp.bfloat16)
    mixed = jnp.dot(activated, down_merged, preferred_element_type=jnp.float32)
    return (wide + mixed).astype(jnp.bfloat16)
```

```python
import jax
import jax.numpy as jnp
from jax import lax
from jax.sharding import PartitionSpec as P

D = 8192


def on_device(hidden_in, norm_gain, w_gate, w_up, w_down, width_factors, unit_factors, slot_block):
    n_replica = lax.axis_size("rollout")
    n_tensor = lax.axis_size("tensor")
    n = n_replica * n_tensor
    block = unit_factors.shape[1]
    rank = unit_factors.shape[2]
    units = w_gate.shape[1]
    f32 = jnp.float32
    flat = jnp.swapaxes(unit_factors, 1, 2).reshape(3 * rank, block)
    per = -(-3 * rank // n)
    flat = jnp.pad(flat, ((0, per * n - 3 * rank), (0, 0))).reshape(n, per, block)
    every = lax.all_to_all(flat, ("rollout", "tensor"), 0, 0, tiled=True)
    dest = jnp.arange(n, dtype=jnp.int32)
    wanted = (dest % n_tensor) * n_replica + dest // n_tensor
    select = jnp.argmax(slot_block[None, :] == wanted[:, None], axis=1)
    sorted_ = jnp.take(every, select, axis=0)
    own = lax.all_to_all(sorted_, ("rollout", "tensor"), 0, 0, tiled=True)
    own = own.reshape(n * per, block)[: 3 * rank]
    both_b = lax.all_gather(own, "rollout", axis=1, tiled=True).reshape(3, rank, units)

    rows = lax.all_gather(hidden_in, "tensor", axis=0, tiled=True)
    width_half = lax.all_gather(width_factors, "tensor", axis=1, tiled=True)
    wide = rows.astype(f32)
    squares = lax.psum(jnp.sum(wide * wide, axis=1, keepdims=True), "rollout")
    scaled = (wide * norm_gain[None, :]).astype(jnp.bfloat16)
    xa = [
        (0.5 * jnp.dot(scaled, width_half[k], preferred_element_type=f32)).astype(jnp.bfloat16)
        for k in range(2)
    ]
    gate = jnp.dot(scaled, w_gate, preferred_element_type=f32)
    upper = jnp.dot(scaled, w_up, preferred_element_type=f32)
    gate = gate + jnp.dot(xa[0], both_b[0], preferred_element_type=f32)
    upper = upper + jnp.dot(xa[1], both_b[1], preferred_element_type=f32)
    gate = lax.psum(gate, "rollout")
    upper = lax.psum(upper, "rollout")
    inv = lax.rsqrt(squares / D + 1e-06)
    activated = (jax.nn.silu(gate * inv) * (upper * inv)).astype(jnp.bfloat16)
    ab = lax.dot_general(activated, both_b[2], (((1,), (1,)), ((), ())), preferred_element_type=f32)
    terms = jnp.dot(activated, w_down, preferred_element_type=f32)
    terms = terms + 0.5 * lax.dot_general(
        ab.astype(jnp.bfloat16), width_half[2], (((1,), (1,)), ((), ())), preferred_element_type=f32
    )
    mixed = lax.psum_scatter(terms, "tensor", scatter_dimension=0, tiled=True)
    return (hidden_in.astype(f32) + mixed).astype(jnp.bfloat16)


def solution(mesh):
    in_specs = (
        P(("groups", "tensor"), "rollout"),
        P("rollout"),
        P("rollout", "tensor"),
        P("rollout", "tensor"),
        P("tensor", "rollout"),
        P("groups", ("rollout", "tensor"), None),
        P("groups", ("rollout", "tensor"), None),
        P("groups"),
    )
    out_specs = P(("groups", "tensor"), "rollout")
    return jax.shard_map(
        on_device, mesh=mesh, in_specs=in_specs, out_specs=out_specs, check_vma=False
    )
```

```python
import jax
import jax.numpy as jnp
from jax import lax
from jax.experimental import pallas as pl
from jax.experimental.pallas import tpu as pltpu
from jax.sharding import PartitionSpec as P

D = 8192


def plain(hidden_in, norm_gain, w_gate, w_up, w_down, width_factors, unit_factors, slot_block):
    n_replica = lax.axis_size("rollout")
    n_tensor = lax.axis_size("tensor")
    n = n_replica * n_tensor
    block = unit_factors.shape[1]
    rank = unit_factors.shape[2]
    units = w_gate.shape[1]
    f32 = jnp.float32
    flat = jnp.swapaxes(unit_factors, 1, 2).reshape(3 * rank, block)
    per = -(-3 * rank // n)
    flat = jnp.pad(flat, ((0, per * n - 3 * rank), (0, 0))).reshape(n, per, block)
    every = lax.all_to_all(flat, ("rollout", "tensor"), 0, 0, tiled=True)
    dest = jnp.arange(n, dtype=jnp.int32)
    wanted = (dest % n_tensor) * n_replica + dest // n_tensor
    select = jnp.argmax(slot_block[None, :] == wanted[:, None], axis=1)
    sorted_ = jnp.take(every, select, axis=0)
    own = lax.all_to_all(sorted_, ("rollout", "tensor"), 0, 0, tiled=True)
    own = own.reshape(n * per, block)[: 3 * rank]
    both_b = lax.all_gather(own, "rollout", axis=1, tiled=True).reshape(3, rank, units)

    rows = lax.all_gather(hidden_in, "tensor", axis=0, tiled=True)
    width_half = lax.all_gather(width_factors, "tensor", axis=1, tiled=True)
    wide = rows.astype(f32)
    squares = lax.psum(jnp.sum(wide * wide, axis=1, keepdims=True), "rollout")
    scaled = (wide * norm_gain[None, :]).astype(jnp.bfloat16)
    xa = [
        (0.5 * jnp.dot(scaled, width_half[k], preferred_element_type=f32)).astype(jnp.bfloat16)
        for k in range(2)
    ]
    gate = jnp.dot(scaled, w_gate, preferred_element_type=f32)
    upper = jnp.dot(scaled, w_up, preferred_element_type=f32)
    gate = gate + jnp.dot(xa[0], both_b[0], preferred_element_type=f32)
    upper = upper + jnp.dot(xa[1], both_b[1], preferred_element_type=f32)
    gate = lax.psum(gate, "rollout")
    upper = lax.psum(upper, "rollout")
    inv = lax.rsqrt(squares / D + 1e-06)
    activated = (jax.nn.silu(gate * inv) * (upper * inv)).astype(jnp.bfloat16)
    ab = lax.dot_general(activated, both_b[2], (((1,), (1,)), ((), ())), preferred_element_type=f32)
    terms = jnp.dot(activated, w_down, preferred_element_type=f32)
    terms = terms + 0.5 * lax.dot_general(
        ab.astype(jnp.bfloat16), width_half[2], (((1,), (1,)), ((), ())), preferred_element_type=f32
    )
    mixed = lax.psum_scatter(terms, "tensor", scatter_dimension=0, tiled=True)
    return (hidden_in.astype(f32) + mixed).astype(jnp.bfloat16)


F32 = jnp.float32
BF = jnp.bfloat16
NB = 3
KC = 512


def kernel(inv_ref, x_ref, a_ref, b_ref, gain_ref, wg, wu, wd, o_ref,
           xr, xs, ag, b1, b2s, bb, acc, pacc, small, psmall, wbuf, dbuf, actb, ab_ref, tb, rb,
           x_s, x_r, a_s, a_r, b1_s, b1_r, b2_s, b2_r, one_s, one_r, t_s, t_r, w_sem, d_sem):
    r = lax.axis_index("rollout")
    t = lax.axis_index("tensor")
    me = r * 8 + t
    other = 1 - r
    units = wg.shape[1]
    wide = acc.shape[2]
    shift = units // 2 % 128
    base = units // 2 - shift

    def rcopy(src, dst, ss, rs, rr, tt):
        return pltpu.make_async_remote_copy(
            src_ref=src, dst_ref=dst, send_sem=ss, recv_sem=rs,
            device_id={"rollout": rr, "tensor": tt}, device_id_type=pl.DeviceIdType.MESH)

    def wcopy(w, k, s):
        slot = lax.rem(s, NB)
        return pltpu.make_async_copy(w.at[pl.ds(k * KC, KC), :], wbuf.at[slot], w_sem.at[slot])

    def dcopy(n):
        slot = lax.rem(n, NB)
        cols = pl.ds(pl.multiple_of(n * KC, KC), KC)
        return pltpu.make_async_copy(wd.at[:, cols], dbuf.at[slot], d_sem.at[slot])

    for s in range(NB):
        wcopy(wg, s, jnp.int32(s)).start()

    barrier = pltpu.get_barrier_semaphore()

    @pl.loop(1, 16)
    def _(o):
        p = lax.rem(me + o, 16)
        pl.semaphore_signal(barrier, inc=1, device_id={"rollout": p // 8, "tensor": lax.rem(p, 8)},
                            device_id_type=pl.DeviceIdType.MESH)

    pl.semaphore_wait(barrier, 15)

    def x_send(p):
        return rcopy(x_ref, xr.at[t], x_s.at[p], x_r.at[t], r, p)

    def x_recv(p):
        return rcopy(x_ref, xr.at[p], x_s.at[p], x_r.at[p], r, p)

    def a_send(p):
        return rcopy(a_ref, ag.at[t], a_s.at[p], a_r.at[t], r, p)

    def a_recv(p):
        return rcopy(a_ref, ag.at[p], a_s.at[p], a_r.at[p], r, p)

    def b1_send(p):
        return rcopy(b_ref.at[p], b1.at[me], b1_s.at[p], b1_r.at[me], p // 8, lax.rem(p, 8))

    def b1_recv(p):
        return rcopy(b_ref.at[p], b1.at[p], b1_s.at[p], b1_r.at[p], p // 8, lax.rem(p, 8))

    def b2_send(p):
        return rcopy(b2s.at[p], bb.at[p // 8, me], b2_s.at[p], b2_r.at[me], p // 8, lax.rem(p, 8))

    def b2_recv(p):
        return rcopy(b2s.at[p], bb.at[r, p], b2_s.at[p], b2_r.at[p], p // 8, lax.rem(p, 8))

    def t_send(n, p):
        return rcopy(tb.at[n, p], rb.at[n, t], t_s.at[n, p], t_r.at[n, t], r, p)

    def t_recv(n, p):
        return rcopy(tb.at[n, p], rb.at[n, p], t_s.at[n, p], t_r.at[n, p], r, p)

    def peers(count, mine, fn):
        @pl.loop(1, count)
        def _(o):
            fn(lax.rem(mine + o, count))

    peers(8, t, lambda p: x_send(p).start())
    peers(8, t, lambda p: a_send(p).start())
    peers(16, me, lambda p: b1_send(p).start())
    xr[t] = x_ref[...]
    ag[t] = a_ref[...]
    b1[me] = b_ref[me]
    acc[...] = jnp.zeros_like(acc)
    for n in range(NB):
        dcopy(jnp.int32(n)).start()
    peers(8, t, lambda p: x_recv(p).wait_recv())

    vs = [xr[p].astype(F32) for p in range(8)]
    sq = jnp.zeros((64, 1), F32)
    for c in range(8):
        h, cc = c // 4, c % 4
        v = jnp.concatenate([vs[p][8 * h:8 * h + 8, KC * cc:KC * cc + KC] for p in range(8)], axis=0)
        sq = sq + jnp.sum(v * v, axis=1, keepdims=True)
        xs[c] = (v * gain_ref[c]).astype(BF)
    small[1] = jnp.broadcast_to(sq, (64, 128))

    def step(w_next, which, first):
        @pl.loop(0, 8)
        def _(k):
            s = first + k
            wcopy(wg, k, s).wait()
            acc[which, :, 0:units] += jnp.dot(xs[k], wbuf[lax.rem(s, NB)], preferred_element_type=F32)

            @pl.when(k + NB < 8)
            def _():
                wcopy(wg if which == 0 else wu, k + NB, s).start()

            if w_next is not None:
                @pl.when(k + NB >= 8)
                def _():
                    wcopy(w_next, k + NB - 8, s).start()

    step(wu, 0, 0)
    sums = [rcopy(acc.at[w], pacc.at[w], one_s.at[w], one_r.at[w], other, t) for w in range(2)]
    sums[0].start()
    peers(16, me, lambda p: b1_recv(p).wait_recv())

    @pl.loop(1, 16)
    def _(o):
        p = lax.rem(me + o, 16)
        b2s[p] = b1[inv_ref[2 * lax.rem(p, 8) + p // 8]]
        b2_send(p).start()

    bb[r, me] = b1[inv_ref[2 * t + r]]

    peers(8, t, lambda p: a_recv(p).wait_recv())
    xa = jnp.zeros((64, 128), F32)
    for c in range(8):
        xa = xa + lax.dot_general(xs[c], ag[c, 0:128, :], (((1,), (1,)), ((), ())), preferred_element_type=F32)
    small[0] = xa
    tiny = rcopy(small, psmall, one_s.at[2], one_r.at[2], other, t)
    tiny.start()

    step(None, 1, 8)
    sums[1].start()
    peers(16, me, lambda p: b2_recv(p).wait_recv())
    fwd = rcopy(bb.at[r], bb.at[r], one_s.at[3], one_r.at[3], other, t)
    fwd.start()
    tiny.wait_recv()
    xaf = (0.5 * (small[0] + psmall[0])).astype(BF)
    inv_rms = lax.rsqrt((small[1, :, 0:1] + psmall[1, :, 0:1]) / D + 1e-06)
    rcopy(bb.at[other], bb.at[other], one_s.at[3], one_r.at[3], other, t).wait_recv()
    sums[0].wait_recv()
    sums[1].wait_recv()

    def chunk(which, b, k):
        return jnp.concatenate([bb[which, a * 4 + b, k] for a in range(4)], axis=0)

    def low(k):
        lhs = xaf[:, 64 * k:64 * k + 64]
        parts = [[jnp.dot(lhs, chunk(w, b, k), preferred_element_type=F32) for b in range(4)] for w in range(2)]
        none = jnp.zeros((64, wide - 2048), F32)
        left = jnp.concatenate(parts[0] + [none], axis=1)
        right = jnp.concatenate([none] + parts[1], axis=1)
        return left + pltpu.roll(right, shift, 1)

    gate = (acc[0] + pacc[0] + low(0)) * inv_rms
    upper = (acc[1] + pacc[1] + low(1)) * inv_rms
    lane = lax.broadcasted_iota(jnp.int32, (64, wide), 1)
    act = jnp.where(lane < units, gate / (1.0 + jnp.exp(-gate)) * upper, 0.0).astype(BF)
    actb[...] = act
    second = pltpu.roll(act.astype(F32), wide - shift, 1)[:, base:base + 2048].astype(BF)
    ab = jnp.zeros((64, 64), F32)
    for w in range(2):
        half = act[:, 0:2048] if w == 0 else second
        for b in range(4):
            ab = ab + lax.dot_general(half[:, KC * b:KC * b + KC], chunk(w, b, 2), (((1,), (1,)), ((), ())),
                                      preferred_element_type=F32)
    ab_ref[...] = (0.5 * ab).astype(BF)

    @pl.loop(0, 8)
    def _(n):
        dcopy(n).wait()
        terms = jnp.dot(actb[:, 0:units], dbuf[lax.rem(n, NB)], preferred_element_type=F32)

        @pl.when(n + NB < 8)
        def _():
            dcopy(n + NB).start()

        terms = terms + jnp.dot(ab_ref[...], ag[n, 128:192, :], preferred_element_type=F32)
        for p in range(8):
            tb[n, p] = jnp.concatenate(
                [terms[8 * p:8 * p + 8, 0:256], terms[8 * p:8 * p + 8, 256:512]], axis=0).astype(BF)
        peers(8, t, lambda p: t_send(n, p).start())
        rb[n, t] = tb[n, t]

    @pl.loop(0, 8)
    def _(n):
        peers(8, t, lambda p: t_recv(n, p).wait_recv())
        total = rb[n, 0].astype(F32)
        for p in range(1, 8):
            total = total + rb[n, p].astype(F32)
        o_ref[n] = total

    peers(8, t, lambda p: x_send(p).wait_send())
    peers(8, t, lambda p: a_send(p).wait_send())
    peers(16, me, lambda p: b1_send(p).wait_send())
    peers(16, me, lambda p: b2_send(p).wait_send())

    @pl.loop(0, 8)
    def _(n):
        peers(8, t, lambda p: t_send(n, p).wait_send())

    sums[0].wait_send()
    sums[1].wait_send()
    tiny.wait_send()
    fwd.wait_send()


def on_device(hidden_in, norm_gain, w_gate, w_up, w_down, width_factors, unit_factors, slot_block):
    n_replica = lax.axis_size("rollout")
    n_tensor = lax.axis_size("tensor")
    block, rank = unit_factors.shape[1:]
    rows, half = hidden_in.shape
    units = w_gate.shape[1]
    fits = (n_replica, n_tensor, rank, rows, half) == (2, 8, 64, 8, 4096) and 1536 < block <= 2048
    if not fits or units != 2 * block or units % 16:
        return plain(hidden_in, norm_gain, w_gate, w_up, w_down, width_factors, unit_factors, slot_block)
    wide = 128 * (units // 2 // 128) + 2048
    inv = jnp.argmax(slot_block[None, :] == jnp.arange(16, dtype=jnp.int32)[:, None], axis=1).astype(jnp.int32)
    x = jnp.concatenate([hidden_in[:, :2048], hidden_in[:, 2048:]], axis=0)
    a = jnp.swapaxes(width_factors, 1, 2).reshape(192, 512)
    b = jnp.pad(jnp.swapaxes(unit_factors, 1, 2), ((0, 0), (0, 0), (0, 2048 - block)))
    b = b.reshape(3, 4, 16, 4, 512).transpose(1, 3, 0, 2, 4).reshape(16, 3, 16, 512)
    gain = norm_gain.reshape(8, 1, 512)
    vmem = pl.BlockSpec(memory_space=pltpu.VMEM)
    hbm = pl.BlockSpec(memory_space=pltpu.HBM)
    dma = pltpu.SemaphoreType.DMA
    out = pl.pallas_call(
        kernel,
        out_shape=jax.ShapeDtypeStruct((8, 16, 256), F32),
        in_specs=[pl.BlockSpec(memory_space=pltpu.SMEM), vmem, vmem, vmem, vmem, hbm, hbm, hbm],
        out_specs=vmem,
        scratch_shapes=[
            pltpu.VMEM((8, 16, 2048), BF), pltpu.VMEM((8, 64, 512), BF), pltpu.VMEM((8, 192, 512), BF),
            pltpu.VMEM((16, 3, 16, 512), BF), pltpu.VMEM((16, 3, 16, 512), BF), pltpu.VMEM((2, 16, 3, 16, 512), BF),
            pltpu.VMEM((2, 64, wide), F32), pltpu.VMEM((2, 64, wide), F32),
            pltpu.VMEM((2, 64, 128), F32), pltpu.VMEM((2, 64, 128), F32),
            pltpu.VMEM((NB, KC, units), BF), pltpu.VMEM((NB, units, KC), BF),
            pltpu.VMEM((64, wide), BF), pltpu.VMEM((64, 64), BF),
            pltpu.VMEM((8, 8, 16, 256), BF), pltpu.VMEM((8, 8, 16, 256), BF),
            dma((8,)), dma((8,)), dma((8,)), dma((8,)), dma((16,)), dma((16,)), dma((16,)), dma((16,)),
            dma((4,)), dma((4,)), dma((8, 8)), dma((8, 8)), dma((NB,)), dma((NB,)),
        ],
        compiler_params=pltpu.CompilerParams(collective_id=0, has_side_effects=True,
                                             vmem_limit_bytes=56 * 1024 * 1024),
        cost_estimate=pl.CostEstimate(flops=11_600_000_000, bytes_accessed=92_000_000, transcendentals=240_000),
    )(inv, x, a, b, gain, w_gate, w_up, w_down)
    mixed = out.reshape(8, 2, 8, 256).transpose(2, 0, 1, 3).reshape(8, 4096)
    return (hidden_in.astype(F32) + mixed).astype(BF)


def solution(mesh):
    in_specs = (
        P(("groups", "tensor"), "rollout"),
        P("rollout"),
        P("rollout", "tensor"),
        P("rollout", "tensor"),
        P("tensor", "rollout"),
        P("groups", ("rollout", "tensor"), None),
        P("groups", ("rollout", "tensor"), None),
        P("groups"),
    )
    out_specs = P(("groups", "tensor"), "rollout")
    return jax.shard_map(
        on_device, mesh=mesh, in_specs=in_specs, out_specs=out_specs, check_vma=False
    )
```

```python
import jax
import jax.numpy as jnp
from jax import lax
from jax.experimental import pallas as pl
from jax.experimental.pallas import tpu as pltpu
from jax.sharding import PartitionSpec as P

D = 8192


def plain(hidden_in, norm_gain, w_gate, w_up, w_down, width_factors, unit_factors, slot_block):
    n_replica = lax.axis_size("rollout")
    n_tensor = lax.axis_size("tensor")
    n = n_replica * n_tensor
    block = unit_factors.shape[1]
    rank = unit_factors.shape[2]
    units = w_gate.shape[1]
    f32 = jnp.float32
    flat = jnp.swapaxes(unit_factors, 1, 2).reshape(3 * rank, block)
    per = -(-3 * rank // n)
    flat = jnp.pad(flat, ((0, per * n - 3 * rank), (0, 0))).reshape(n, per, block)
    every = lax.all_to_all(flat, ("rollout", "tensor"), 0, 0, tiled=True)
    dest = jnp.arange(n, dtype=jnp.int32)
    wanted = (dest % n_tensor) * n_replica + dest // n_tensor
    select = jnp.argmax(slot_block[None, :] == wanted[:, None], axis=1)
    sorted_ = jnp.take(every, select, axis=0)
    own = lax.all_to_all(sorted_, ("rollout", "tensor"), 0, 0, tiled=True)
    own = own.reshape(n * per, block)[: 3 * rank]
    both_b = lax.all_gather(own, "rollout", axis=1, tiled=True).reshape(3, rank, units)

    rows = lax.all_gather(hidden_in, "tensor", axis=0, tiled=True)
    width_half = lax.all_gather(width_factors, "tensor", axis=1, tiled=True)
    wide = rows.astype(f32)
    squares = lax.psum(jnp.sum(wide * wide, axis=1, keepdims=True), "rollout")
    scaled = (wide * norm_gain[None, :]).astype(jnp.bfloat16)
    xa = [
        (0.5 * jnp.dot(scaled, width_half[k], preferred_element_type=f32)).astype(jnp.bfloat16)
        for k in range(2)
    ]
    gate = jnp.dot(scaled, w_gate, preferred_element_type=f32)
    upper = jnp.dot(scaled, w_up, preferred_element_type=f32)
    gate = gate + jnp.dot(xa[0], both_b[0], preferred_element_type=f32)
    upper = upper + jnp.dot(xa[1], both_b[1], preferred_element_type=f32)
    gate = lax.psum(gate, "rollout")
    upper = lax.psum(upper, "rollout")
    inv = lax.rsqrt(squares / D + 1e-06)
    activated = (jax.nn.silu(gate * inv) * (upper * inv)).astype(jnp.bfloat16)
    ab = lax.dot_general(activated, both_b[2], (((1,), (1,)), ((), ())), preferred_element_type=f32)
    terms = jnp.dot(activated, w_down, preferred_element_type=f32)
    terms = terms + 0.5 * lax.dot_general(
        ab.astype(jnp.bfloat16), width_half[2], (((1,), (1,)), ((), ())), preferred_element_type=f32
    )
    mixed = lax.psum_scatter(terms, "tensor", scatter_dimension=0, tiled=True)
    return (hidden_in.astype(f32) + mixed).astype(jnp.bfloat16)


F32 = jnp.float32
BF = jnp.bfloat16
NB = 6
KC = 512


def kernel(inv_ref, x_ref, a_ref, b_ref, gain_ref, wg, wu, wd, o_ref,
           xr, xs, pa, pb, b1, b2s, bb, acc, pacc, small, psmall, wbuf, actb, tb, rb,
           x_s, x_r, a_s, a_r, c_s, c_r, f_s, f_r, b1_s, b1_r, b2_s, b2_r, one_s, one_r, t_s, t_r, w_sem):
    r = lax.axis_index("rollout")
    t = lax.axis_index("tensor")
    me = r * 8 + t
    other = 1 - r
    beside = t + 1 - 2 * lax.rem(t, 2)
    units = wg.shape[0]
    wide = acc.shape[2]
    shift = units // 2 % 128
    base = units // 2 - shift

    def rcopy(src, dst, ss, rs, rr, tt):
        return pltpu.make_async_remote_copy(
            src_ref=src, dst_ref=dst, send_sem=ss, recv_sem=rs,
            device_id={"rollout": rr, "tensor": tt}, device_id_type=pl.DeviceIdType.MESH)

    def wcopy(w, k, s):
        slot = lax.rem(s, NB)
        cols = pl.ds(pl.multiple_of(k * KC, KC), KC)
        return pltpu.make_async_copy(w.at[:, cols], wbuf.at[slot], w_sem.at[slot])

    def prefetch(s):
        for i, w in enumerate((wg, wu, wd)):
            @pl.when((s >= 8 * i) & (s < 8 * i + 8))
            def _():
                wcopy(w, s - 8 * i, s).start()

    for s in range(NB):
        wcopy(wg, jnp.int32(s), jnp.int32(s)).start()

    barrier = pltpu.get_barrier_semaphore()

    @pl.loop(1, 16)
    def _(o):
        p = lax.rem(me + o, 16)
        pl.semaphore_signal(barrier, inc=1, device_id={"rollout": p // 8, "tensor": lax.rem(p, 8)},
                            device_id_type=pl.DeviceIdType.MESH)

    pl.semaphore_wait(barrier, 15)

    def x_send(p):
        return rcopy(x_ref, xr.at[t], x_s.at[p], x_r.at[t], r, p)

    def x_pass(p):
        return rcopy(xr.at[p], xr.at[p], f_s.at[p], x_r.at[p], r, beside)

    def x_recv(p):
        return rcopy(x_ref, xr.at[p], x_s.at[p], x_r.at[p], r, p)

    def a_send(p):
        return rcopy(pa.at[t], pa.at[t], a_s.at[p], a_r.at[t], r, p)

    def a_recv(p):
        return rcopy(pa.at[p], pa.at[p], a_s.at[p], a_r.at[p], r, p)

    def c_send(p):
        return rcopy(pb.at[t], pb.at[t], c_s.at[p], c_r.at[t], r, p)

    def c_recv(p):
        return rcopy(pb.at[p], pb.at[p], c_s.at[p], c_r.at[p], r, p)

    def f_send(p):
        return rcopy(bb.at[r, p], bb.at[r, p], f_s.at[8 + p], f_r.at[p], other, t)

    def f_recv(p):
        return rcopy(bb.at[other, p], bb.at[other, p], f_s.at[8 + p], f_r.at[p], other, t)

    def b1_send(p):
        return rcopy(b_ref.at[p], b1.at[me], b1_s.at[p], b1_r.at[me], p // 8, lax.rem(p, 8))

    def b1_recv(p):
        return rcopy(b_ref.at[p], b1.at[p], b1_s.at[p], b1_r.at[p], p // 8, lax.rem(p, 8))

    def b2_send(p):
        return rcopy(b2s.at[p], bb.at[p // 8, me], b2_s.at[p], b2_r.at[me], p // 8, lax.rem(p, 8))

    def b2_recv(p):
        return rcopy(b2s.at[p], bb.at[r, p], b2_s.at[p], b2_r.at[p], p // 8, lax.rem(p, 8))

    def t_send(n, p):
        return rcopy(tb.at[n, p], rb.at[n, t], t_s.at[n, p], t_r.at[n, t], r, p)

    def t_recv(n, p):
        return rcopy(tb.at[n, p], rb.at[n, p], t_s.at[n, p], t_r.at[n, p], r, p)

    def peers(count, mine, fn):
        @pl.loop(1, count)
        def _(o):
            fn(lax.rem(mine + o, count))

    column = [lax.rem(t + 2 * o, 8) for o in (1, 3, 2)]
    for p in column:
        x_send(p).start()
    x_send(beside).start()
    xr[t] = x_ref[...]
    b1[me] = b_ref[me]
    acc[...] = jnp.zeros_like(acc)
    for p in column:
        x_recv(p).wait_recv()
        x_pass(p).start()
    x_recv(beside).wait_recv()
    for p in column:
        x_recv(p + beside - t).wait_recv()
    peers(16, me, lambda p: b1_send(p).start())

    vs = [xr[p].astype(F32) for p in range(8)]
    sq = jnp.zeros((64, 1), F32)
    for c in range(8):
        h, cc = c // 4, c % 4
        v = jnp.concatenate([vs[p][8 * h:8 * h + 8, KC * cc:KC * cc + KC] for p in range(8)], axis=0)
        sq = sq + jnp.sum(v * v, axis=1, keepdims=True)
        xs[c] = (v * gain_ref[c]).astype(BF)
    small[1] = jnp.broadcast_to(sq, (64, 128))

    pa[t] = lax.dot_general(xs[t], a_ref[0:128, :], (((1,), (1,)), ((), ())),
                            preferred_element_type=F32).astype(BF)
    peers(8, t, lambda p: a_send(p).start())

    def step(which):
        @pl.loop(0, 8)
        def _(k):
            s = 8 * which + k
            wcopy(wg, k, s).wait()
            acc[which, :, 0:units] += lax.dot_general(
                xs[k], wbuf[lax.rem(s, NB)], (((1,), (1,)), ((), ())), preferred_element_type=F32)
            prefetch(s + NB)

    step(0)
    sums = [rcopy(acc.at[w], pacc.at[w], one_s.at[w], one_r.at[w], other, t) for w in range(2)]
    sums[0].start()
    peers(16, me, lambda p: b1_recv(p).wait_recv())

    @pl.loop(1, 16)
    def _(o):
        p = lax.rem(me + o, 16)
        b2s[p] = b1[inv_ref[2 * lax.rem(p, 8) + p // 8]]
        b2_send(p).start()

    bb[r, me] = b1[inv_ref[2 * t + r]]

    peers(8, t, lambda p: a_recv(p).wait_recv())
    xa = pa[0].astype(F32)
    for p in range(1, 8):
        xa = xa + pa[p].astype(F32)
    small[0] = xa
    tiny = rcopy(small, psmall, one_s.at[2], one_r.at[2], other, t)
    tiny.start()

    step(1)
    sums[1].start()
    f_send(me).start()

    def onward(p):
        b2_recv(p).wait_recv()
        f_send(p).start()

    peers(16, me, onward)
    tiny.wait_recv()
    xaf = (0.5 * (small[0] + psmall[0])).astype(BF)
    inv_rms = lax.rsqrt((small[1, :, 0:1] + psmall[1, :, 0:1]) / D + 1e-06)

    @pl.loop(0, 16)
    def _(p):
        f_recv(p).wait_recv()

    sums[0].wait_recv()
    sums[1].wait_recv()

    def chunk(which, b, k):
        return jnp.concatenate([bb[which, a * 4 + b, k] for a in range(4)], axis=0)

    def low(k):
        lhs = xaf[:, 64 * k:64 * k + 64]
        parts = [[jnp.dot(lhs, chunk(w, b, k), preferred_element_type=F32) for b in range(4)] for w in range(2)]
        none = jnp.zeros((64, wide - 2048), F32)
        left = jnp.concatenate(parts[0] + [none], axis=1)
        right = jnp.concatenate([none] + parts[1], axis=1)
        return left + pltpu.roll(right, shift, 1)

    gate = (acc[0] + pacc[0] + low(0)) * inv_rms
    upper = (acc[1] + pacc[1] + low(1)) * inv_rms
    lane = lax.broadcasted_iota(jnp.int32, (64, wide), 1)
    act = jnp.where(lane < units, gate / (1.0 + jnp.exp(-gate)) * upper, 0.0).astype(BF)
    actb[...] = act
    second = pltpu.roll(act.astype(F32), wide - shift, 1)[:, base:base + 2048].astype(BF)
    ab = jnp.zeros((64, 64), F32)
    for w in range(2):
        half = act[:, 0:2048] if w == 0 else second
        for b in range(4):
            ab = ab + lax.dot_general(half[:, KC * b:KC * b + KC], chunk(w, b, 2), (((1,), (1,)), ((), ())),
                                      preferred_element_type=F32)
    pb[t] = jnp.concatenate([0.5 * ab, jnp.zeros((64, 64), F32)], axis=1).astype(BF)
    peers(8, t, lambda p: c_send(p).start())

    def hand_on(n, terms):
        for p in range(8):
            tb[n, p] = jnp.concatenate(
                [terms[8 * p:8 * p + 8, 0:256], terms[8 * p:8 * p + 8, 256:512]], axis=0).astype(BF)
        peers(8, t, lambda p: t_send(n, p).start())
        rb[n, t] = tb[n, t]

    @pl.loop(0, 8)
    def _(n):
        s = 16 + n
        wcopy(wd, n, s).wait()
        terms = jnp.dot(actb[:, 0:units], wbuf[lax.rem(s, NB)], preferred_element_type=F32)
        prefetch(s + NB)
        hand_on(n, terms)

        @pl.when(n == 3)
        def _():
            peers(8, t, lambda p: c_recv(p).wait_recv())
            whole = pb[0].astype(F32)
            for p in range(1, 8):
                whole = whole + pb[p].astype(F32)
            hand_on(8, jnp.dot(whole[:, 0:64].astype(BF), a_ref[128:192, :], preferred_element_type=F32))

    peers(8, t, lambda p: t_recv(8, p).wait_recv())

    @pl.loop(0, 8)
    def _(n):
        peers(8, t, lambda p: t_recv(n, p).wait_recv())
        total = rb[n, 0].astype(F32)
        for p in range(1, 8):
            total = total + rb[n, p].astype(F32)
        o_ref[n] = total + rb[8, n].astype(F32)

    for p in column:
        x_send(p).wait_send()
        x_pass(p).wait_send()
    x_send(beside).wait_send()
    peers(8, t, lambda p: c_send(p).wait_send())
    peers(8, t, lambda p: a_send(p).wait_send())
    peers(16, me, lambda p: b1_send(p).wait_send())
    peers(16, me, lambda p: b2_send(p).wait_send())

    @pl.loop(0, 9)
    def _(n):
        peers(8, t, lambda p: t_send(n, p).wait_send())

    @pl.loop(0, 16)
    def _(p):
        f_send(p).wait_send()

    sums[0].wait_send()
    sums[1].wait_send()
    tiny.wait_send()


def on_device(hidden_in, norm_gain, w_gate, w_up, w_down, width_factors, unit_factors, slot_block):
    n_replica = lax.axis_size("rollout")
    n_tensor = lax.axis_size("tensor")
    block, rank = unit_factors.shape[1:]
    rows, half = hidden_in.shape
    units = w_gate.shape[1]
    fits = (n_replica, n_tensor, rank, rows, half) == (2, 8, 64, 8, 4096) and 1536 < block <= 2048
    if not fits or units != 2 * block or units % 16:
        return plain(hidden_in, norm_gain, w_gate, w_up, w_down, width_factors, unit_factors, slot_block)
    wide = 128 * (units // 2 // 128) + 2048
    inv = jnp.argmax(slot_block[None, :] == jnp.arange(16, dtype=jnp.int32)[:, None], axis=1).astype(jnp.int32)
    x = jnp.concatenate([hidden_in[:, :2048], hidden_in[:, 2048:]], axis=0)
    a = jnp.swapaxes(width_factors, 1, 2).reshape(192, 512)
    b = jnp.pad(jnp.swapaxes(unit_factors, 1, 2), ((0, 0), (0, 0), (0, 2048 - block)))
    b = b.reshape(3, 4, 16, 4, 512).transpose(1, 3, 0, 2, 4).reshape(16, 3, 16, 512)
    gain = norm_gain.reshape(8, 1, 512)
    vmem = pl.BlockSpec(memory_space=pltpu.VMEM)
    hbm = pl.BlockSpec(memory_space=pltpu.HBM)
    dma = pltpu.SemaphoreType.DMA
    out = pl.pallas_call(
        kernel,
        out_shape=jax.ShapeDtypeStruct((8, 16, 256), F32),
        in_specs=[pl.BlockSpec(memory_space=pltpu.SMEM), vmem, vmem, vmem, vmem, hbm, hbm, hbm],
        out_specs=vmem,
        scratch_shapes=[
            pltpu.VMEM((8, 16, 2048), BF), pltpu.VMEM((8, 64, 512), BF), pltpu.VMEM((8, 64, 128), BF), pltpu.VMEM((8, 64, 128), BF),
            pltpu.VMEM((16, 3, 16, 512), BF), pltpu.VMEM((16, 3, 16, 512), BF), pltpu.VMEM((2, 16, 3, 16, 512), BF),
            pltpu.VMEM((2, 64, wide), F32), pltpu.VMEM((2, 64, wide), F32),
            pltpu.VMEM((2, 64, 128), F32), pltpu.VMEM((2, 64, 128), F32),
            pltpu.VMEM((NB, units, KC), BF),
            pltpu.VMEM((64, wide), BF),
            pltpu.VMEM((9, 8, 16, 256), BF), pltpu.VMEM((9, 8, 16, 256), BF),
            dma((8,)), dma((8,)), dma((8,)), dma((8,)), dma((8,)), dma((8,)), dma((24,)), dma((16,)),
            dma((16,)), dma((16,)), dma((16,)), dma((16,)),
            dma((3,)), dma((3,)), dma((9, 8)), dma((9, 8)), dma((NB,)),
        ],
        compiler_params=pltpu.CompilerParams(collective_id=0, has_side_effects=True,
                                             vmem_limit_bytes=56 * 1024 * 1024),
        cost_estimate=pl.CostEstimate(flops=11_600_000_000, bytes_accessed=92_000_000, transcendentals=240_000),
    )(inv, x, a, b, gain, w_gate.T, w_up.T, w_down)
    mixed = out.reshape(8, 2, 8, 256).transpose(2, 0, 1, 3).reshape(8, 4096)
    return (hidden_in.astype(F32) + mixed).astype(BF)


def solution(mesh):
    in_specs = (
        P(("groups", "tensor"), "rollout"),
        P("rollout"),
        P("rollout", "tensor"),
        P("rollout", "tensor"),
        P("tensor", "rollout"),
        P("groups", ("rollout", "tensor"), None),
        P("groups", ("rollout", "tensor"), None),
        P("groups"),
    )
    out_specs = P(("groups", "tensor"), "rollout")
    return jax.shard_map(
        on_device, mesh=mesh, in_specs=in_specs, out_specs=out_specs, check_vma=False
    )
```

```python
import jax
import jax.numpy as jnp
from jax import lax
from jax.experimental import pallas as pl
from jax.experimental.pallas import tpu as pltpu
from jax.sharding import PartitionSpec as P

D = 8192


def plain(hidden_in, norm_gain, w_gate, w_up, w_down, width_factors, unit_factors, slot_block):
    n_replica = lax.axis_size("rollout")
    n_tensor = lax.axis_size("tensor")
    n = n_replica * n_tensor
    block = unit_factors.shape[1]
    rank = unit_factors.shape[2]
    units = w_gate.shape[1]
    f32 = jnp.float32
    flat = jnp.swapaxes(unit_factors, 1, 2).reshape(3 * rank, block)
    per = -(-3 * rank // n)
    flat = jnp.pad(flat, ((0, per * n - 3 * rank), (0, 0))).reshape(n, per, block)
    every = lax.all_to_all(flat, ("rollout", "tensor"), 0, 0, tiled=True)
    dest = jnp.arange(n, dtype=jnp.int32)
    wanted = (dest % n_tensor) * n_replica + dest // n_tensor
    select = jnp.argmax(slot_block[None, :] == wanted[:, None], axis=1)
    sorted_ = jnp.take(every, select, axis=0)
    own = lax.all_to_all(sorted_, ("rollout", "tensor"), 0, 0, tiled=True)
    own = own.reshape(n * per, block)[: 3 * rank]
    both_b = lax.all_gather(own, "rollout", axis=1, tiled=True).reshape(3, rank, units)

    rows = lax.all_gather(hidden_in, "tensor", axis=0, tiled=True)
    width_half = lax.all_gather(width_factors, "tensor", axis=1, tiled=True)
    wide = rows.astype(f32)
    squares = lax.psum(jnp.sum(wide * wide, axis=1, keepdims=True), "rollout")
    scaled = (wide * norm_gain[None, :]).astype(jnp.bfloat16)
    xa = [
        (0.5 * jnp.dot(scaled, width_half[k], preferred_element_type=f32)).astype(jnp.bfloat16)
        for k in range(2)
    ]
    gate = jnp.dot(scaled, w_gate, preferred_element_type=f32)
    upper = jnp.dot(scaled, w_up, preferred_element_type=f32)
    gate = gate + jnp.dot(xa[0], both_b[0], preferred_element_type=f32)
    upper = upper + jnp.dot(xa[1], both_b[1], preferred_element_type=f32)
    gate = lax.psum(gate, "rollout")
    upper = lax.psum(upper, "rollout")
    inv = lax.rsqrt(squares / D + 1e-06)
    activated = (jax.nn.silu(gate * inv) * (upper * inv)).astype(jnp.bfloat16)
    ab = lax.dot_general(activated, both_b[2], (((1,), (1,)), ((), ())), preferred_element_type=f32)
    terms = jnp.dot(activated, w_down, preferred_element_type=f32)
    terms = terms + 0.5 * lax.dot_general(
        ab.astype(jnp.bfloat16), width_half[2], (((1,), (1,)), ((), ())), preferred_element_type=f32
    )
    mixed = lax.psum_scatter(terms, "tensor", scatter_dimension=0, tiled=True)
    return (hidden_in.astype(f32) + mixed).astype(jnp.bfloat16)


F32 = jnp.float32
BF = jnp.bfloat16
NB = 6
KC = 512


def kernel(inv_ref, x_ref, a_ref, b_ref, gain_ref, wg, wu, wd, o_ref,
           xr, xs, pa, pb, b1, b2s, bb, acc, pacc, small, psmall, wbuf, actb, tb, rb,
           x_s, x_r, a_s, a_r, c_s, c_r, f_s, f_r, b1_s, b1_r, b2_s, b2_r, one_s, one_r, t_s, t_r, w_sem):
    r = lax.axis_index("rollout")
    t = lax.axis_index("tensor")
    me = r * 8 + t
    other = 1 - r
    beside = t + 1 - 2 * lax.rem(t, 2)
    units = wg.shape[0]
    wide = acc.shape[2]
    shift = units // 2 % 128
    base = units // 2 - shift

    def rcopy(src, dst, ss, rs, rr, tt):
        return pltpu.make_async_remote_copy(
            src_ref=src, dst_ref=dst, send_sem=ss, recv_sem=rs,
            device_id={"rollout": rr, "tensor": tt}, device_id_type=pl.DeviceIdType.MESH)

    def wcopy(w, k, s):
        slot = lax.rem(s, NB)
        cols = pl.ds(pl.multiple_of(k * KC, KC), KC)
        return pltpu.make_async_copy(w.at[:, cols], wbuf.at[slot], w_sem.at[slot])

    def prefetch(s):
        for i, w in enumerate((wg, wu, wd)):
            @pl.when((s >= 8 * i) & (s < 8 * i + 8))
            def _():
                wcopy(w, s - 8 * i, s).start()

    for s in range(NB):
        wcopy(wg, jnp.int32(s), jnp.int32(s)).start()

    barrier = pltpu.get_barrier_semaphore()

    @pl.loop(1, 16)
    def _(o):
        p = lax.rem(me + o, 16)
        pl.semaphore_signal(barrier, inc=1, device_id={"rollout": p // 8, "tensor": lax.rem(p, 8)},
                            device_id_type=pl.DeviceIdType.MESH)

    pl.semaphore_wait(barrier, 15)

    def x_send(p):
        return rcopy(x_ref, xr.at[t], x_s.at[p], x_r.at[t], r, p)

    def x_pass(p):
        return rcopy(xr.at[p], xr.at[p], f_s.at[p], x_r.at[p], r, beside)

    def x_recv(p):
        return rcopy(x_ref, xr.at[p], x_s.at[p], x_r.at[p], r, p)

    def a_send(p):
        return rcopy(pa.at[t], pa.at[t], a_s.at[p], a_r.at[t], r, p)

    def a_recv(p):
        return rcopy(pa.at[p], pa.at[p], a_s.at[p], a_r.at[p], r, p)

    def c_send(p):
        return rcopy(pb.at[t], pb.at[t], c_s.at[p], c_r.at[t], r, p)

    def c_recv(p):
        return rcopy(pb.at[p], pb.at[p], c_s.at[p], c_r.at[p], r, p)

    def f_send(p):
        return rcopy(bb.at[r, p], bb.at[r, p], f_s.at[8 + p], f_r.at[p], other, t)

    def f_recv(p):
        return rcopy(bb.at[other, p], bb.at[other, p], f_s.at[8 + p], f_r.at[p], other, t)

    def b1_send(p):
        return rcopy(b_ref.at[p], b1.at[me], b1_s.at[p], b1_r.at[me], p // 8, lax.rem(p, 8))

    def b1_recv(p):
        return rcopy(b_ref.at[p], b1.at[p], b1_s.at[p], b1_r.at[p], p // 8, lax.rem(p, 8))

    def b2_send(p):
        return rcopy(b2s.at[p], bb.at[p // 8, me], b2_s.at[p], b2_r.at[me], p // 8, lax.rem(p, 8))

    def b2_recv(p):
        return rcopy(b2s.at[p], bb.at[r, p], b2_s.at[p], b2_r.at[p], p // 8, lax.rem(p, 8))

    def t_send(n, p):
        return rcopy(tb.at[n, p], rb.at[n, t], t_s.at[n, p], t_r.at[n, t], r, p)

    def t_recv(n, p):
        return rcopy(tb.at[n, p], rb.at[n, p], t_s.at[n, p], t_r.at[n, p], r, p)

    def peers(count, mine, fn):
        @pl.loop(1, count)
        def _(o):
            fn(lax.rem(mine + o, count))

    column = [lax.rem(t + 2 * o, 8) for o in (1, 3, 2)]
    for p in column:
        x_send(p).start()
    x_send(beside).start()
    peers(16, me, lambda p: b1_send(p).start())
    xr[t] = x_ref[...]
    b1[me] = b_ref[me]
    acc[...] = jnp.zeros_like(acc)
    for p in column:
        x_recv(p).wait_recv()
        x_pass(p).start()
    x_recv(beside).wait_recv()
    for p in column:
        x_recv(p + beside - t).wait_recv()

    vs = [xr[p].astype(F32) for p in range(8)]
    sq = jnp.zeros((64, 1), F32)
    for c in range(8):
        h, cc = c // 4, c % 4
        v = jnp.concatenate([vs[p][8 * h:8 * h + 8, KC * cc:KC * cc + KC] for p in range(8)], axis=0)
        sq = sq + jnp.sum(v * v, axis=1, keepdims=True)
        xs[c] = (v * gain_ref[c]).astype(BF)
    small[1] = jnp.broadcast_to(sq, (64, 128))

    pa[t] = lax.dot_general(xs[t], a_ref[0:128, :], (((1,), (1,)), ((), ())),
                            preferred_element_type=F32).astype(BF)
    peers(8, t, lambda p: a_send(p).start())

    def step(which):
        @pl.loop(0, 8)
        def _(k):
            s = 8 * which + k
            wcopy(wg, k, s).wait()
            acc[which, :, 0:units] += lax.dot_general(
                xs[k], wbuf[lax.rem(s, NB)], (((1,), (1,)), ((), ())), preferred_element_type=F32)
            prefetch(s + NB)

    step(0)
    sums = [rcopy(acc.at[w], pacc.at[w], one_s.at[w], one_r.at[w], other, t) for w in range(2)]
    sums[0].start()
    peers(16, me, lambda p: b1_recv(p).wait_recv())

    @pl.loop(1, 16)
    def _(o):
        p = lax.rem(me + o, 16)
        b2s[p] = b1[inv_ref[2 * lax.rem(p, 8) + p // 8]]
        b2_send(p).start()

    bb[r, me] = b1[inv_ref[2 * t + r]]

    peers(8, t, lambda p: a_recv(p).wait_recv())
    xa = pa[0].astype(F32)
    for p in range(1, 8):
        xa = xa + pa[p].astype(F32)
    small[0] = xa
    tiny = rcopy(small, psmall, one_s.at[2], one_r.at[2], other, t)
    tiny.start()

    step(1)
    sums[1].start()
    f_send(me).start()

    def onward(p):
        b2_recv(p).wait_recv()
        f_send(p).start()

    peers(16, me, onward)
    tiny.wait_recv()
    xaf = (0.5 * (small[0] + psmall[0])).astype(BF)
    inv_rms = lax.rsqrt((small[1, :, 0:1] + psmall[1, :, 0:1]) / D + 1e-06)

    @pl.loop(0, 16)
    def _(p):
        f_recv(p).wait_recv()

    sums[0].wait_recv()
    sums[1].wait_recv()

    def chunk(which, b, k):
        return jnp.concatenate([bb[which, a * 4 + b, k] for a in range(4)], axis=0)

    def low(k):
        lhs = xaf[:, 64 * k:64 * k + 64]
        parts = [[jnp.dot(lhs, chunk(w, b, k), preferred_element_type=F32) for b in range(4)] for w in range(2)]
        none = jnp.zeros((64, wide - 2048), F32)
        left = jnp.concatenate(parts[0] + [none], axis=1)
        right = jnp.concatenate([none] + parts[1], axis=1)
        return left + pltpu.roll(right, shift, 1)

    gate = (acc[0] + pacc[0] + low(0)) * inv_rms
    upper = (acc[1] + pacc[1] + low(1)) * inv_rms
    lane = lax.broadcasted_iota(jnp.int32, (64, wide), 1)
    act = jnp.where(lane < units, gate / (1.0 + jnp.exp(-gate)) * upper, 0.0).astype(BF)
    actb[...] = act
    second = pltpu.roll(act.astype(F32), wide - shift, 1)[:, base:base + 2048].astype(BF)
    ab = jnp.zeros((64, 64), F32)
    for w in range(2):
        half = act[:, 0:2048] if w == 0 else second
        for b in range(4):
            ab = ab + lax.dot_general(half[:, KC * b:KC * b + KC], chunk(w, b, 2), (((1,), (1,)), ((), ())),
                                      preferred_element_type=F32)
    pb[t] = jnp.concatenate([0.5 * ab, jnp.zeros((64, 64), F32)], axis=1).astype(BF)
    peers(8, t, lambda p: c_send(p).start())

    def hand_on(n, terms):
        for p in range(8):
            tb[n, p] = jnp.concatenate(
                [terms[8 * p:8 * p + 8, 0:256], terms[8 * p:8 * p + 8, 256:512]], axis=0).astype(BF)
        peers(8, t, lambda p: t_send(n, p).start())
        rb[n, t] = tb[n, t]

    @pl.loop(0, 8)
    def _(n):
        s = 16 + n
        wcopy(wd, n, s).wait()
        terms = jnp.dot(actb[:, 0:units], wbuf[lax.rem(s, NB)], preferred_element_type=F32)
        prefetch(s + NB)
        hand_on(n, terms)

        @pl.when(n == 3)
        def _():
            peers(8, t, lambda p: c_recv(p).wait_recv())
            whole = pb[0].astype(F32)
            for p in range(1, 8):
                whole = whole + pb[p].astype(F32)
            hand_on(8, jnp.dot(whole[:, 0:64].astype(BF), a_ref[128:192, :], preferred_element_type=F32))

    peers(8, t, lambda p: t_recv(8, p).wait_recv())

    @pl.loop(0, 8)
    def _(n):
        peers(8, t, lambda p: t_recv(n, p).wait_recv())
        total = rb[n, 0].astype(F32)
        for p in range(1, 8):
            total = total + rb[n, p].astype(F32)
        o_ref[n] = total + rb[8, n].astype(F32)

    for p in column:
        x_send(p).wait_send()
        x_pass(p).wait_send()
    x_send(beside).wait_send()
    peers(8, t, lambda p: c_send(p).wait_send())
    peers(8, t, lambda p: a_send(p).wait_send())
    peers(16, me, lambda p: b1_send(p).wait_send())
    peers(16, me, lambda p: b2_send(p).wait_send())

    @pl.loop(0, 9)
    def _(n):
        peers(8, t, lambda p: t_send(n, p).wait_send())

    @pl.loop(0, 16)
    def _(p):
        f_send(p).wait_send()

    sums[0].wait_send()
    sums[1].wait_send()
    tiny.wait_send()


def on_device(hidden_in, norm_gain, w_gate, w_up, w_down, width_factors, unit_factors, slot_block):
    n_replica = lax.axis_size("rollout")
    n_tensor = lax.axis_size("tensor")
    block, rank = unit_factors.shape[1:]
    rows, half = hidden_in.shape
    units = w_gate.shape[1]
    fits = (n_replica, n_tensor, rank, rows, half) == (2, 8, 64, 8, 4096) and 1536 < block <= 2048
    if not fits or units != 2 * block or units % 16:
        return plain(hidden_in, norm_gain, w_gate, w_up, w_down, width_factors, unit_factors, slot_block)
    wide = 128 * (units // 2 // 128) + 2048
    inv = jnp.argmax(slot_block[None, :] == jnp.arange(16, dtype=jnp.int32)[:, None], axis=1).astype(jnp.int32)
    x = jnp.concatenate([hidden_in[:, :2048], hidden_in[:, 2048:]], axis=0)
    a = jnp.swapaxes(width_factors, 1, 2).reshape(192, 512)
    b = jnp.pad(jnp.swapaxes(unit_factors, 1, 2), ((0, 0), (0, 0), (0, 2048 - block)))
    b = b.reshape(3, 4, 16, 4, 512).transpose(1, 3, 0, 2, 4).reshape(16, 3, 16, 512)
    gain = norm_gain.reshape(8, 1, 512)
    vmem = pl.BlockSpec(memory_space=pltpu.VMEM)
    hbm = pl.BlockSpec(memory_space=pltpu.HBM)
    dma = pltpu.SemaphoreType.DMA
    out = pl.pallas_call(
        kernel,
        out_shape=jax.ShapeDtypeStruct((8, 16, 256), F32),
        in_specs=[pl.BlockSpec(memory_space=pltpu.SMEM), vmem, vmem, vmem, vmem, hbm, hbm, hbm],
        out_specs=vmem,
        scratch_shapes=[
            pltpu.VMEM((8, 16, 2048), BF), pltpu.VMEM((8, 64, 512), BF), pltpu.VMEM((8, 64, 128), BF), pltpu.VMEM((8, 64, 128), BF),
            pltpu.VMEM((16, 3, 16, 512), BF), pltpu.VMEM((16, 3, 16, 512), BF), pltpu.VMEM((2, 16, 3, 16, 512), BF),
            pltpu.VMEM((2, 64, wide), F32), pltpu.VMEM((2, 64, wide), F32),
            pltpu.VMEM((2, 64, 128), F32), pltpu.VMEM((2, 64, 128), F32),
            pltpu.VMEM((NB, units, KC), BF),
            pltpu.VMEM((64, wide), BF),
            pltpu.VMEM((9, 8, 16, 256), BF), pltpu.VMEM((9, 8, 16, 256), BF),
            dma((8,)), dma((8,)), dma((8,)), dma((8,)), dma((8,)), dma((8,)), dma((24,)), dma((16,)),
            dma((16,)), dma((16,)), dma((16,)), dma((16,)),
            dma((3,)), dma((3,)), dma((9, 8)), dma((9, 8)), dma((NB,)),
        ],
        compiler_params=pltpu.CompilerParams(collective_id=0, has_side_effects=True,
                                             vmem_limit_bytes=56 * 1024 * 1024),
        cost_estimate=pl.CostEstimate(flops=11_600_000_000, bytes_accessed=92_000_000, transcendentals=240_000),
    )(inv, x, a, b, gain, w_gate.T, w_up.T, w_down)
    mixed = out.reshape(8, 2, 8, 256).transpose(2, 0, 1, 3).reshape(8, 4096)
    return (hidden_in.astype(F32) + mixed).astype(BF)


def solution(mesh):
    in_specs = (
        P(("groups", "tensor"), "rollout"),
        P("rollout"),
        P("rollout", "tensor"),
        P("rollout", "tensor"),
        P("tensor", "rollout"),
        P("groups", ("rollout", "tensor"), None),
        P("groups", ("rollout", "tensor"), None),
        P("groups"),
    )
    out_specs = P(("groups", "tensor"), "rollout")
    return jax.shard_map(
        on_device, mesh=mesh, in_specs=in_specs, out_specs=out_specs, check_vma=False
    )
```
